32 devices in a mesh: row: 4 (over x, core), col: 8 (over z, y).
Axes of the slice: x: 2, y: 2, z: 4, core: 2. Of those that a mesh axis runs over, the one named last changes fastest.
Arguments:
- a_blocks: bfloat16 [4, 8, 24, 4096], P('row', 'col'), may hold values from -1.1953125 to 1.1953125
- b_blocks: bfloat16 [4, 8, 24, 4096], P('row', 'col'), may hold values from -1.1953125 to 1.1953125
- products: int32 [4, 8, 2, 3, 384], P('row', 'col'), may hold values from 0 to 32, as said below
Outputs:
- product: float32 [4, 8, 32, 4096], P('row', 'col')
- norm_sq: float32 [], replicated
The draws below stay inside these ranges and needn't reach their ends.
Inputs may be any that keep to these rules, and one draw needn't show every extreme that they name: `products`: left and right slots lie below 24; a product slot of 32 marks an unused entry; in every draw some grid position uses all 384 entries in some step, and every position uses at least a third of them.
All inputs are finite; a program needn't handle non-finite values.
Results may differ from the reference program's by a relative error of at most 0.0003.
Values may be sent and summed in bfloat16 or wider, within the bound.
No kernel may reach another device: no remote copies, remote signals or barrier semaphores. Data moves between devices by JAX's collectives and lax.ppermute only.
A program may use at most 64 MiB of HBM per device.

```python
import jax
import jax.numpy as jnp
from jax import lax

BS = 64
NNZ = 24
NC = 32
NPROD = 384
N_ROW = 4
N_COL = 8


def draw_products(key, part):
    key = jax.random.fold_in(key, 7)
    keys = jax.random.split(key, 5)
    shape = (N_ROW, N_COL, 2, NPROD)
    left_slot = jax.random.randint(keys[0], shape, 0, NNZ)
    right_slot = jax.random.randint(keys[1], shape, 0, NNZ)
    out_slot = jax.random.randint(keys[2], shape, 0, NC)
    live = jax.random.randint(keys[3], (N_ROW * N_COL * 2,), NPROD // 3, NPROD + 1)
    full_at = jax.random.randint(keys[4], (), 0, N_ROW * N_COL * 2)
    live = jnp.where(jnp.arange(N_ROW * N_COL * 2) == full_at, NPROD, live).reshape(N_ROW, N_COL, 2, 1)
    used = jnp.arange(NPROD).reshape(1, 1, 1, NPROD) < live
    out_slot = jnp.where(used, out_slot, NC)
    return jnp.stack([left_slot, right_slot, out_slot], axis=3).astype(jnp.int32)


def shard_levels(key, dims, cuts, least, largest):
    factor_of = 1.0
    for position, blocks in cuts:
        steps = jax.random.uniform(jax.random.fold_in(jax.random.fold_in(key, 6), position), (blocks,), jnp.float32, least / len(cuts), largest / len(cuts))
        factor_of = factor_of * jnp.repeat(jnp.exp(steps), dims[position] // blocks).reshape((-1,) + (1,) * (len(dims) - 1 - position))
    return factor_of


def bell_draw(rng, shape, deviation, most, shards=(), kind=jnp.bfloat16):
    level = shard_levels(rng, shape, shards, -0.22, 0.18) if shards else 1.0
    values = jax.random.normal(rng, shape, jnp.float32) * deviation * level
    return jnp.minimum(jnp.maximum(values, -most), most).astype(kind)


def setup_inputs(seed: int = 0) -> dict:
    streams_of = jax.random.split(jax.random.key(seed), 4)
    a_blocks = bell_draw(streams_of[0], (N_ROW, N_COL, NNZ, BS * BS), 0.18, 1.1953125, ((0, 4), (1, 8)))
    b_blocks = bell_draw(streams_of[1], (N_ROW, N_COL, NNZ, BS * BS), 0.18, 1.1953125, ((0, 4), (1, 8)))
    products = draw_products(jax.random.fold_in(streams_of[3], 71), 0)
    return {"a_blocks": a_blocks, "b_blocks": b_blocks, "products": products}


def multiply(left_tile, right_tile, slots):
    left = left_tile.reshape(-1, BS, BS)[slots[0]].astype(jnp.float32)
    right = right_tile.reshape(-1, BS, BS)[slots[1]].astype(jnp.float32)
    blocks = jnp.einsum('pik,pkj->pij', left, right).reshape(-1, BS * BS)
    return jax.ops.segment_sum(blocks, slots[2], num_segments=NC)


def reference(a_blocks, b_blocks, products):
    a_next = jnp.roll(a_blocks, -1, axis=1)
    b_next = jnp.roll(b_blocks, -1, axis=0)
    count = N_ROW * N_COL

    def flatten(array):
        return array.reshape((count,) + array.shape[2:])

    def one_device(inputs):
        a_here, b_here, a_there, b_there, slots = inputs
        total = multiply(a_here, b_here, slots[0]) + multiply(a_there, b_there, slots[1])
        squares = jnp.sum(jnp.square(a_here.astype(jnp.float32)))
        return total, squares

    totals, squares = lax.map(one_device, (flatten(a_blocks), flatten(b_blocks), flatten(a_next), flatten(b_next), flatten(products)))
    product = totals.reshape(N_ROW, N_COL, NC, BS * BS)
    norm_sq = jnp.sum(squares) / jnp.float32(N_ROW * N_COL * NNZ * BS)
    return product, norm_sq
```

```python
import functools

import jax
import jax.numpy as jnp
from jax import lax
from jax.experimental import pallas as pl
from jax.experimental.pallas import tpu as pltpu
from jax.sharding import PartitionSpec as P

BS = 64
NNZ = 24
NC = 32
LANES = 128
PAIRS = BS * BS // LANES
UNROLL = 8


def passed_along(block, axis, distance):
    devices = range(lax.axis_size(axis))
    route = [((i - distance) % len(devices), i) for i in devices]
    return lax.ppermute(block, axis, route)


def norm_kernel(a_ref, out_ref):
    x = a_ref[0, 0].astype(jnp.float32)
    x = x * x
    total = x[:, :LANES]
    for t in range(1, PAIRS):
        total = total + x[:, t * LANES : (t + 1) * LANES]
    row = jnp.sum(total, axis=0, keepdims=True)
    out_ref[...] = jnp.broadcast_to(row[None], out_ref.shape)


def step_kernel(step, a_ref, b_ref, slots_ref, *rest):
    if step == 0:
        out_ref, wide, left, pairs = rest
        total = out_ref
    else:
        before_ref, out_ref, wide, left, pairs, total = rest
    low = lax.broadcasted_iota(jnp.int32, (NNZ, LANES), 1) < BS

    for t in range(PAIRS):
        wide[pl.ds(t, NNZ, stride=PAIRS), :] = a_ref[0, 0, :, t * LANES : (t + 1) * LANES].astype(jnp.float32)
    left[...] = wide[: NNZ * PAIRS, :].astype(jnp.bfloat16)

    for t in range(PAIRS):
        x = b_ref[0, 0, :, t * LANES : (t + 1) * LANES].astype(jnp.float32)
        swapped = pltpu.roll(x, BS, 1)
        wide[pl.ds(2 * t, NNZ, stride=BS), :] = jnp.where(low, x, swapped)
        wide[pl.ds(2 * t + 1, NNZ, stride=BS), :] = jnp.where(low, swapped, x)

    side = lax.broadcasted_iota(jnp.int32, (BS, LANES), 1) < BS

    def all_pairs(p, carry):
        weights = []
        for q in range(2):
            x = wide[pl.ds(pl.multiple_of((2 * p + q) * BS, BS), BS), :]
            weights.append(
                jnp.concatenate([jnp.where(side, x, 0.0), jnp.where(side, 0.0, x)], axis=0).astype(jnp.bfloat16)
            )
        result = jnp.dot(left[...], jnp.concatenate(weights, axis=1), preferred_element_type=jnp.float32)
        for q in range(2):
            pairs[pl.ds((2 * p + q) * NNZ, NNZ)] = result[:, q * LANES : (q + 1) * LANES].reshape(NNZ, PAIRS, LANES)
        return carry

    lax.fori_loop(0, NNZ // 2, all_pairs, 0)

    if step == 0:
        total[...] = jnp.zeros_like(total)
    else:
        total[...] = before_ref[...]

    count = slots_ref.shape[-1]

    def add_entries(i, carry):
        for u in range(UNROLL):
            e = i * UNROLL + u
            at = slots_ref[0, 0, step, 1, e] * NNZ + slots_ref[0, 0, step, 0, e]
            to = slots_ref[0, 0, step, 2, e]
            total[to] = total[to] + pairs[at]
        return carry

    lax.fori_loop(0, count // UNROLL, add_entries, 0)

    if step == 1:
        flat = total.reshape((NC + 1) * PAIRS, LANES)
        for t in range(PAIRS):
            out_ref[0, 0, :, t * LANES : (t + 1) * LANES] = flat[pl.ds(t, NC, stride=PAIRS), :]


VMEM = pl.BlockSpec(memory_space=pltpu.VMEM)
SMEM = pl.BlockSpec(memory_space=pltpu.SMEM)


def accumulate(step, a_blocks, b_blocks, products, before=None):
    held = jax.ShapeDtypeStruct((NC + 1, PAIRS, LANES), jnp.float32)
    scratch = [
        pltpu.VMEM((NNZ * BS, LANES), jnp.float32),
        pltpu.VMEM((NNZ * PAIRS, LANES), jnp.bfloat16),
        pltpu.VMEM((NNZ * NNZ, PAIRS, LANES), jnp.float32),
    ]
    if step == 1:
        scratch.append(pltpu.VMEM(held.shape, held.dtype))
        result = jax.ShapeDtypeStruct((1, 1, NC, BS * BS), jnp.float32)
        operands = (a_blocks, b_blocks, products, before)
    else:
        result = held
        operands = (a_blocks, b_blocks, products)
    return pl.pallas_call(
        functools.partial(step_kernel, step),
        out_shape=result,
        in_specs=[VMEM, VMEM, SMEM] + [VMEM] * step,
        out_specs=VMEM,
        scratch_shapes=scratch,
        compiler_params=pltpu.CompilerParams(vmem_limit_bytes=32 * 1024 * 1024),
        cost_estimate=pl.CostEstimate(flops=6 * 10**8, bytes_accessed=4 * 10**6, transcendentals=0),
        name=f"step_{step}",
    )(*operands)


def global_squares(a_blocks):
    count = lax.axis_size("row") * lax.axis_size("col")
    mine = pl.pallas_call(
        norm_kernel,
        out_shape=jax.ShapeDtypeStruct((count, 1, LANES), jnp.float32),
        in_specs=[VMEM],
        out_specs=VMEM,
        name="squares",
    )(a_blocks)
    everyone = lax.all_to_all(mine, ("row", "col"), 0, 0, tiled=True)
    return jnp.sum(everyone) * jnp.float32(1.0 / (count * NNZ * BS))


def per_device(a_blocks, b_blocks, products):
    a_moved = passed_along(a_blocks, "col", -1)
    b_moved = passed_along(b_blocks, "row", -1)
    norm_sq = global_squares(a_blocks)
    first = accumulate(0, a_blocks, b_blocks, products)
    product = accumulate(1, a_moved, b_moved, products, first)
    return (product, norm_sq)


def solution(mesh):
    return jax.shard_map(
        per_device,
        mesh=mesh,
        in_specs=(
            P("row", "col", None, None),
            P("row", "col", None, None),
            P("row", "col", None, None, None),
        ),
        out_specs=(P("row", "col", None, None), P()),
        check_vma=False,
    )
```

```python
import functools

import jax
import jax.numpy as jnp
from jax import lax
from jax.experimental import pallas as pl
from jax.experimental.pallas import tpu as pltpu
from jax.sharding import PartitionSpec as P

BS = 64
NNZ = 24
NC = 32
LANES = 128
PAIRS = BS * BS // LANES
UNROLL = 16
TOTALS = 4
SHIFT = 11


def passed_along(block, axis, distance):
    devices = range(lax.axis_size(axis))
    route = [((i - distance) % len(devices), i) for i in devices]
    return lax.ppermute(block, axis, route)


def norm_kernel(a_ref, out_ref):
    x = a_ref[0, 0].astype(jnp.float32)
    x = x * x
    total = x[:, :LANES]
    for t in range(1, PAIRS):
        total = total + x[:, t * LANES : (t + 1) * LANES]
    row = jnp.sum(total, axis=0, keepdims=True)
    out_ref[...] = jnp.broadcast_to(row[None], out_ref.shape)


def step_kernel(step, a_ref, b_ref, slots_ref, *rest):
    if step == 0:
        out_ref, listed, places, wide, left, pairs, *totals, sem = rest
    else:
        before_ref, out_ref, listed, places, wide, left, pairs, *totals, sem = rest

    slots = slots_ref[0, 0, step]
    listed[...] = ((slots[1:2] * NNZ + slots[0:1]) * (PAIRS << SHIFT)) + slots[2:3] * PAIRS
    copy = pltpu.make_async_copy(listed, places, sem)
    copy.start()

    for t in range(PAIRS):
        wide[pl.ds(t, NNZ, stride=PAIRS), :] = a_ref[0, 0, :, t * LANES : (t + 1) * LANES].astype(jnp.float32)
    left[...] = wide[: NNZ * PAIRS, :].astype(jnp.bfloat16)

    low = lax.broadcasted_iota(jnp.int32, (NNZ, LANES), 1) < BS
    for t in range(PAIRS):
        x = b_ref[0, 0, :, t * LANES : (t + 1) * LANES].astype(jnp.float32)
        swapped = pltpu.roll(x, BS, 1)
        wide[pl.ds(2 * t, NNZ, stride=BS), :] = jnp.where(low, x, swapped)
        wide[pl.ds(2 * t + 1, NNZ, stride=BS), :] = jnp.where(low, swapped, x)

    for total in totals:
        total[...] = jnp.zeros_like(total)
    if step == 1:
        totals[0][...] = before_ref[...]

    side = lax.broadcasted_iota(jnp.int32, (BS, LANES), 1) < BS
    for p in range(NNZ // 2):
        weights = []
        for r in (2 * p, 2 * p + 1):
            x = wide[r * BS : (r + 1) * BS, :]
            weights.append(
                jnp.concatenate([jnp.where(side, x, 0.0), jnp.where(side, 0.0, x)], axis=0).astype(jnp.bfloat16)
            )
        result = jnp.dot(left[...], jnp.concatenate(weights, axis=1), preferred_element_type=jnp.float32)
        rows = NNZ * PAIRS
        for q in range(2):
            pairs[(2 * p + q) * rows : (2 * p + q + 1) * rows, :] = result[:, q * LANES : (q + 1) * LANES]

    copy.wait()

    def add_entries(i, carry):
        for u in range(UNROLL):
            place = places[0, i * UNROLL + u]
            at = pl.multiple_of(lax.shift_right_logical(place, SHIFT), PAIRS)
            to = pl.multiple_of(place & ((1 << SHIFT) - 1), PAIRS)
            total = totals[u % len(totals)]
            total[pl.ds(to, PAIRS), :] = total[pl.ds(to, PAIRS), :] + pairs[pl.ds(at, PAIRS), :]
        return carry

    lax.fori_loop(0, places.shape[1] // UNROLL, add_entries, 0)

    if step == 0:
        rows = out_ref.shape[0]
        out_ref[...] = (totals[0][:rows] + totals[1][:rows]) + (totals[2][:rows] + totals[3][:rows])
    else:
        for t in range(PAIRS):
            row = [total[pl.ds(t, NC, stride=PAIRS), :] for total in totals]
            out_ref[0, 0, :, t * LANES : (t + 1) * LANES] = (row[0] + row[1]) + (row[2] + row[3])


VMEM = pl.BlockSpec(memory_space=pltpu.VMEM)


def accumulate(step, a_blocks, b_blocks, products, before=None):
    held = jax.ShapeDtypeStruct(((NC + 1) * PAIRS, LANES), jnp.float32)
    count = products.shape[-1]
    if step == 1:
        result = jax.ShapeDtypeStruct((1, 1, NC, BS * BS), jnp.float32)
        operands = (a_blocks, b_blocks, products, before)
    else:
        result = held
        operands = (a_blocks, b_blocks, products)
    return pl.pallas_call(
        functools.partial(step_kernel, step),
        out_shape=result,
        in_specs=[VMEM] * len(operands),
        out_specs=VMEM,
        scratch_shapes=[
            pltpu.VMEM((1, count), jnp.int32),
            pltpu.SMEM((1, count), jnp.int32),
            pltpu.VMEM((NNZ * BS, LANES), jnp.float32),
            pltpu.VMEM((NNZ * PAIRS, LANES), jnp.bfloat16),
            pltpu.VMEM((NNZ * NNZ * PAIRS, LANES), jnp.float32),
        ]
        + [pltpu.VMEM(held.shape, held.dtype)] * TOTALS
        + [pltpu.SemaphoreType.DMA],
        compiler_params=pltpu.CompilerParams(vmem_limit_bytes=32 * 1024 * 1024),
        cost_estimate=pl.CostEstimate(flops=6 * 10**8, bytes_accessed=4 * 10**6, transcendentals=0),
        name=f"step_{step}",
    )(*operands)


def global_squares(a_blocks):
    count = lax.axis_size("row") * lax.axis_size("col")
    mine = pl.pallas_call(
        norm_kernel,
        out_shape=jax.ShapeDtypeStruct((count, 1, LANES), jnp.float32),
        in_specs=[VMEM],
        out_specs=VMEM,
        name="squares",
    )(a_blocks)
    everyone = lax.all_to_all(mine, ("row", "col"), 0, 0, tiled=True)
    return jnp.sum(everyone * jnp.float32(1.0 / (count * NNZ * BS)))


def per_device(a_blocks, b_blocks, products):
    a_moved = passed_along(a_blocks, "col", -1)
    b_moved = passed_along(b_blocks, "row", -1)
    norm_sq = global_squares(a_blocks)
    first = accumulate(0, a_blocks, b_blocks, products)
    product = accumulate(1, a_moved, b_moved, products, first)
    return (product, norm_sq)


def solution(mesh):
    return jax.shard_map(
        per_device,
        mesh=mesh,
        in_specs=(
            P("row", "col", None, None),
            P("row", "col", None, None),
            P("row", "col", None, None, None),
        ),
        out_specs=(P("row", "col", None, None), P()),
        check_vma=False,
    )
```

```python
import jax
import jax.numpy as jnp
from jax import lax
from jax.experimental import pallas as pl
from jax.experimental.pallas import tpu as pltpu
from jax.sharding import PartitionSpec as P

BS = 64
NNZ = 24
NC = 32
LANES = 128
PAIRS = BS * BS // LANES
PAD = 8
APART = PAIRS + PAD
UNROLL = 16
TOTALS = 4
SHIFT = 11

VMEM = pl.BlockSpec(memory_space=pltpu.VMEM)


def passed_along(block, axis, distance):
    devices = range(lax.axis_size(axis))
    route = [((i - distance) % len(devices), i) for i in devices]
    return lax.ppermute(block, axis, route)


def squares_kernel(a_ref, out_ref):
    total = jnp.zeros((NNZ, LANES), jnp.float32)
    for t in range(PAIRS):
        x = a_ref[0, 0, :, t * LANES : (t + 1) * LANES].astype(jnp.float32)
        total = total + x * x
    row = jnp.sum(total, axis=0, keepdims=True)
    out_ref[...] = jnp.broadcast_to(row[None], out_ref.shape)


def send_list(slots_ref, step, listed, place, sem):
    left_slot, right_slot, product_slot = (slots_ref[0, 0, kind, step : step + 1] for kind in range(3))
    listed[...] = (right_slot * NNZ + left_slot) * (PAIRS << SHIFT) + product_slot * APART
    copy = pltpu.make_async_copy(listed.at[0], place, sem)
    copy.start()
    return copy


def add_products(a_ref, b_ref, places, arriving, wide, left, pairs, totals):
    for t in range(PAIRS):
        wide[pl.ds(t, NNZ, stride=APART), :] = a_ref[0, 0, :, t * LANES : (t + 1) * LANES].astype(jnp.float32)
    for n in range(NNZ):
        left[n * PAIRS : (n + 1) * PAIRS, :] = wide[n * APART : n * APART + PAIRS, :].astype(jnp.bfloat16)

    low = lax.broadcasted_iota(jnp.int32, (NNZ, LANES), 1) < BS
    for t in range(PAIRS):
        x = b_ref[0, 0, :, t * LANES : (t + 1) * LANES].astype(jnp.float32)
        swapped = pltpu.roll(x, BS, 1)
        wide[pl.ds(2 * t, NNZ, stride=BS + PAD), :] = jnp.where(low, x, swapped)
        wide[pl.ds(2 * t + 1, NNZ, stride=BS + PAD), :] = jnp.where(low, swapped, x)

    side = lax.broadcasted_iota(jnp.int32, (BS, LANES), 1) < BS
    for p in range(NNZ // 2):
        weights = []
        for r in (2 * p, 2 * p + 1):
            x = wide[r * (BS + PAD) : r * (BS + PAD) + BS, :]
            weights.append(
                jnp.concatenate([jnp.where(side, x, 0.0), jnp.where(side, 0.0, x)], axis=0).astype(jnp.bfloat16)
            )
        result = jnp.dot(left[...], jnp.concatenate(weights, axis=1), preferred_element_type=jnp.float32)
        rows = NNZ * PAIRS
        for q in range(2):
            pairs[(2 * p + q) * rows : (2 * p + q + 1) * rows, :] = result[:, q * LANES : (q + 1) * LANES]

    arriving.wait()

    def add_entries(i, carry):
        for u in range(UNROLL):
            place = places[i * UNROLL + u]
            at = pl.multiple_of(lax.shift_right_logical(place, SHIFT), PAIRS)
            to = pl.multiple_of(place & ((1 << SHIFT) - 1), PAD)
            total = totals[u % TOTALS]
            total[pl.ds(to, PAIRS), :] = total[pl.ds(to, PAIRS), :] + pairs[pl.ds(at, PAIRS), :]
        return carry

    lax.fori_loop(0, places.shape[0] // UNROLL, add_entries, 0)


def moved_kernel(a_ref, b_ref, slots_ref, *rest):
    totals = rest[:TOTALS]
    listed, place, wide, left, pairs, sem = rest[TOTALS:]

    copy = send_list(slots_ref, 1, listed, place, sem)
    for total in totals:
        total[...] = jnp.zeros_like(total)
    add_products(a_ref, b_ref, place, copy, wide, left, pairs, totals)


def own_kernel(a_ref, b_ref, slots_ref, *rest):
    _, out_ref, totals = rest[:TOTALS], rest[TOTALS], rest[TOTALS + 1 : 2 * TOTALS + 1]
    listed, place, wide, left, pairs, sem = rest[2 * TOTALS + 1 :]
    copy = send_list(slots_ref, 0, listed, place, sem)
    add_products(a_ref, b_ref, place, copy, wide, left, pairs, totals)

    for c in range(NC):
        rows = slice(c * APART, c * APART + PAIRS)
        totals[0][rows] = (totals[0][rows] + totals[1][rows]) + (totals[2][rows] + totals[3][rows])
    for t in range(PAIRS):
        out_ref[0, 0, :, t * LANES : (t + 1) * LANES] = totals[0][pl.ds(t, NC, stride=APART), :]


def both_products(a_blocks, b_blocks, a_moved, b_moved, products):
    count = products.shape[-1]
    slots = jnp.swapaxes(products, 2, 3)
    total = jax.ShapeDtypeStruct(((NC + 1) * APART, LANES), jnp.float32)
    work = [
        pltpu.VMEM((1, count), jnp.int32),
        pltpu.SMEM((count,), jnp.int32),
        pltpu.VMEM((NNZ * (BS + PAD), LANES), jnp.float32),
        pltpu.VMEM((NNZ * PAIRS, LANES), jnp.bfloat16),
        pltpu.VMEM((NNZ * NNZ * PAIRS, LANES), jnp.float32),
        pltpu.SemaphoreType.DMA,
    ]
    settings = dict(
        compiler_params=pltpu.CompilerParams(vmem_limit_bytes=32 * 1024 * 1024),
        cost_estimate=pl.CostEstimate(flops=6 * 10**8, bytes_accessed=4 * 10**6, transcendentals=0),
    )
    totals = pl.pallas_call(
        moved_kernel,
        out_shape=(total,) * TOTALS,
        in_specs=[VMEM] * 3,
        out_specs=(VMEM,) * TOTALS,
        scratch_shapes=work,
        name="moved",
        **settings,
    )(a_moved, b_moved, slots)
    return pl.pallas_call(
        own_kernel,
        out_shape=(jax.ShapeDtypeStruct((1, 1, NC, BS * BS), jnp.float32),) + (total,) * TOTALS,
        in_specs=[VMEM] * (3 + TOTALS),
        out_specs=(VMEM,) * (1 + TOTALS),
        scratch_shapes=work,
        input_output_aliases={3 + i: 1 + i for i in range(TOTALS)},
        name="own",
        **settings,
    )(a_blocks, b_blocks, slots, *totals)[0]


def spread_squares(a_blocks):
    count = lax.axis_size("row") * lax.axis_size("col")
    mine = pl.pallas_call(
        squares_kernel,
        out_shape=jax.ShapeDtypeStruct((count, 1, LANES), jnp.float32),
        in_specs=[VMEM],
        out_specs=VMEM,
        name="squares",
    )(a_blocks)
    everyone = lax.all_to_all(mine, ("row", "col"), 0, 0, tiled=True)
    return everyone, jnp.float32(1.0 / (count * NNZ * BS))


def per_device(a_blocks, b_blocks, products):
    a_moved = passed_along(a_blocks, "col", -1)
    b_moved = passed_along(b_blocks, "row", -1)
    everyone, scale = spread_squares(a_blocks)
    product = both_products(a_blocks, b_blocks, a_moved, b_moved, products)
    everyone, product = lax.optimization_barrier((everyone, product))
    norm_sq = jnp.sum(everyone * scale)
    return (product, norm_sq)


def solution(mesh):
    return jax.shard_map(
        per_device,
        mesh=mesh,
        in_specs=(
            P("row", "col", None, None),
            P("row", "col", None, None),
            P("row", "col", None, None, None),
        ),
        out_specs=(P("row", "col", None, None), P()),
        check_vma=False,
    )
```

```python
import functools

import jax
import jax.numpy as jnp
from jax import lax
from jax.experimental import pallas as pl
from jax.experimental.pallas import tpu as pltpu
from jax.sharding import PartitionSpec as P

BS = 64
NNZ = 24
NC = 32
LANES = 128
PAIRS = BS * BS // LANES
PAD = 8
APART = PAIRS + PAD
UNROLL = 16
TOTALS = 4
SHIFT = 11
PREPARE_VMEM = 66450000

VMEM = pl.BlockSpec(memory_space=pltpu.VMEM)
ANY = pl.BlockSpec(memory_space=pl.ANY)


def passed_along(block, axis, distance):
    devices = range(lax.axis_size(axis))
    route = [((i - distance) % len(devices), i) for i in devices]
    return lax.ppermute(block, axis, route)


def prepare_kernel(first_column, a_ref, b_ref, *rest):
    squares_ref, a_near, b_near, spread, a_sem, b_sem, out_sem = rest[-7:]
    at_start = lax.axis_index("col") == 0

    @pl.when(at_start if first_column else jnp.logical_not(at_start))
    def _():
        a_copy = pltpu.make_async_copy(a_ref, a_near, a_sem)
        b_copy = pltpu.make_async_copy(b_ref, b_near, b_sem)
        a_copy.start()
        b_copy.start()
        a_copy.wait()
        total = jnp.zeros((NNZ, LANES), jnp.float32)
        for t in range(PAIRS):
            x = a_near[0, 0, :, t * LANES : (t + 1) * LANES].astype(jnp.float32)
            total = total + x * x
        row = jnp.sum(total, axis=0, keepdims=True)
        spread[...] = jnp.broadcast_to(row[None], spread.shape)
        out_copy = pltpu.make_async_copy(spread, squares_ref, out_sem)
        out_copy.start()
        b_copy.wait()
        out_copy.wait()


def send_list(slots_ref, step, listed, place, sem):
    left_slot, right_slot, product_slot = (slots_ref[0, 0, kind, step : step + 1] for kind in range(3))
    listed[...] = (right_slot * NNZ + left_slot) * (PAIRS << SHIFT) + product_slot * APART
    copy = pltpu.make_async_copy(listed.at[0], place, sem)
    copy.start()
    return copy


def add_products(a_ref, b_ref, places, arriving, wide, left, pairs, totals):
    for t in range(PAIRS):
        wide[pl.ds(t, NNZ, stride=APART), :] = a_ref[0, 0, :, t * LANES : (t + 1) * LANES].astype(jnp.float32)
    for n in range(NNZ):
        left[n * PAIRS : (n + 1) * PAIRS, :] = wide[n * APART : n * APART + PAIRS, :].astype(jnp.bfloat16)

    low = lax.broadcasted_iota(jnp.int32, (NNZ, LANES), 1) < BS
    for t in range(PAIRS):
        x = b_ref[0, 0, :, t * LANES : (t + 1) * LANES].astype(jnp.float32)
        swapped = pltpu.roll(x, BS, 1)
        wide[pl.ds(2 * t, NNZ, stride=BS + PAD), :] = jnp.where(low, x, swapped)
        wide[pl.ds(2 * t + 1, NNZ, stride=BS + PAD), :] = jnp.where(low, swapped, x)

    side = lax.broadcasted_iota(jnp.int32, (BS, LANES), 1) < BS
    for p in range(NNZ // 2):
        weights = []
        for r in (2 * p, 2 * p + 1):
            x = wide[r * (BS + PAD) : r * (BS + PAD) + BS, :]
            weights.append(
                jnp.concatenate([jnp.where(side, x, 0.0), jnp.where(side, 0.0, x)], axis=0).astype(jnp.bfloat16)
            )
        result = jnp.dot(left[...], jnp.concatenate(weights, axis=1), preferred_element_type=jnp.float32)
        rows = NNZ * PAIRS
        for q in range(2):
            pairs[(2 * p + q) * rows : (2 * p + q + 1) * rows, :] = result[:, q * LANES : (q + 1) * LANES]

    arriving.wait()

    def add_entries(i, carry):
        for u in range(UNROLL):
            place = places[i * UNROLL + u]
            at = pl.multiple_of(lax.shift_right_logical(place, SHIFT), PAIRS)
            to = pl.multiple_of(place & ((1 << SHIFT) - 1), PAD)
            total = totals[u % TOTALS]
            total[pl.ds(to, PAIRS), :] = total[pl.ds(to, PAIRS), :] + pairs[pl.ds(at, PAIRS), :]
        return carry

    lax.fori_loop(0, places.shape[0] // UNROLL, add_entries, 0)


def own_kernel(a_ref, b_ref, slots_ref, *rest):
    totals = rest[:TOTALS]
    listed, place, wide, left, pairs, sem = rest[TOTALS:]
    copy = send_list(slots_ref, 0, listed, place, sem)
    for total in totals:
        total[...] = jnp.zeros_like(total)
    add_products(a_ref, b_ref, place, copy, wide, left, pairs, totals)


def moved_kernel(a_ref, b_ref, slots_ref, *rest):
    _, out_ref, totals = rest[:TOTALS], rest[TOTALS], rest[TOTALS + 1 : 2 * TOTALS + 1]
    listed, place, wide, left, pairs, sem = rest[2 * TOTALS + 1 :]
    copy = send_list(slots_ref, 1, listed, place, sem)
    add_products(a_ref, b_ref, place, copy, wide, left, pairs, totals)

    for c in range(NC):
        rows = slice(c * APART, c * APART + PAIRS)
        totals[0][rows] = (totals[0][rows] + totals[1][rows]) + (totals[2][rows] + totals[3][rows])
    for t in range(PAIRS):
        out_ref[0, 0, :, t * LANES : (t + 1) * LANES] = totals[0][pl.ds(t, NC, stride=APART), :]


def both_products(a_blocks, b_blocks, a_moved, b_moved, products):
    count = products.shape[-1]
    slots = jnp.swapaxes(products, 2, 3)
    total = jax.ShapeDtypeStruct(((NC + 1) * APART, LANES), jnp.float32)
    settings = dict(
        scratch_shapes=[
            pltpu.VMEM((1, count), jnp.int32),
            pltpu.SMEM((count,), jnp.int32),
            pltpu.VMEM((NNZ * (BS + PAD), LANES), jnp.float32),
            pltpu.VMEM((NNZ * PAIRS, LANES), jnp.bfloat16),
            pltpu.VMEM((NNZ * NNZ * PAIRS, LANES), jnp.float32),
            pltpu.SemaphoreType.DMA,
        ],
        compiler_params=pltpu.CompilerParams(vmem_limit_bytes=32 * 1024 * 1024),
        cost_estimate=pl.CostEstimate(flops=6 * 10**8, bytes_accessed=4 * 10**6, transcendentals=0),
    )
    totals = pl.pallas_call(
        own_kernel,
        out_shape=(total,) * TOTALS,
        in_specs=[VMEM] * 3,
        out_specs=(VMEM,) * TOTALS,
        name="own",
        **settings,
    )(a_blocks, b_blocks, slots)
    return pl.pallas_call(
        moved_kernel,
        out_shape=(jax.ShapeDtypeStruct((1, 1, NC, BS * BS), jnp.float32),) + (total,) * TOTALS,
        in_specs=[VMEM] * (3 + TOTALS),
        out_specs=(VMEM,) * (1 + TOTALS),
        input_output_aliases={3 + i: 1 + i for i in range(TOTALS)},
        name="moved",
        **settings,
    )(a_moved, b_moved, slots, *totals)[0]


def prepare(a_blocks, b_blocks, count, before=()):
    first_column = not before
    return pl.pallas_call(
        functools.partial(prepare_kernel, first_column),
        out_shape=(
            jax.ShapeDtypeStruct((count, 1, LANES), jnp.float32),
            pltpu.VMEM(a_blocks.shape, a_blocks.dtype),
            pltpu.VMEM(b_blocks.shape, b_blocks.dtype),
        ),
        in_specs=[ANY, ANY] + [ANY, VMEM, VMEM][: len(before)],
        out_specs=(ANY, VMEM, VMEM),
        scratch_shapes=[pltpu.VMEM((count, 1, LANES), jnp.float32)] + [pltpu.SemaphoreType.DMA] * 3,
        input_output_aliases={} if first_column else {2: 0, 3: 1, 4: 2},
        compiler_params=pltpu.CompilerParams(vmem_limit_bytes=PREPARE_VMEM) if first_column else None,
        name="prepare_early" if first_column else "prepare_late",
    )(
        pltpu.with_memory_space_constraint(a_blocks, pltpu.HBM),
        pltpu.with_memory_space_constraint(b_blocks, pltpu.HBM),
        *before,
    )


def per_device(a_blocks, b_blocks, products):
    count = lax.axis_size("row") * lax.axis_size("col")
    ready = prepare(a_blocks, b_blocks, count)
    *ready, a_after = lax.optimization_barrier((*ready, a_blocks))
    a_moved = passed_along(a_after, "col", -1)
    b_moved = passed_along(b_blocks, "row", -1)
    squares, a_near, b_near = prepare(a_blocks, b_blocks, count, tuple(ready))
    everyone = lax.all_to_all(squares, ("row", "col"), 0, 0, tiled=True)
    product = both_products(a_near, b_near, a_moved, b_moved, products)
    everyone, product = lax.optimization_barrier((everyone, product))
    norm_sq = jnp.sum(everyone * jnp.float32(1.0 / (count * NNZ * BS)))
    return (product, norm_sq)


def solution(mesh):
    return jax.shard_map(
        per_device,
        mesh=mesh,
        in_specs=(
            P("row", "col", None, None),
            P("row", "col", None, None),
            P("row", "col", None, None, None),
        ),
        out_specs=(P("row", "col", None, None), P()),
        check_vma=False,
    )
```

```python
import functools

import jax
import jax.numpy as jnp
from jax import lax
from jax.experimental import pallas as pl
from jax.experimental.pallas import tpu as pltpu
from jax.sharding import PartitionSpec as P

BS = 64
NNZ = 24
NC = 32
LANES = 128
PAIRS = BS * BS // LANES
PAD = 8
APART = PAIRS + PAD
UNROLL = 16
TOTALS = 4
SHIFT = 11
FULL_VMEM = 66900000
SOME_VMEM = 16 * 1024 * 1024

VMEM = pl.BlockSpec(memory_space=pltpu.VMEM)
ANY = pl.BlockSpec(memory_space=pl.ANY)


def passed_along(block, axis, distance):
    devices = range(lax.axis_size(axis))
    route = [((i - distance) % len(devices), i) for i in devices]
    return lax.ppermute(block, axis, route)


def squares_kernel(first_column, a_ref, *rest):
    out_ref, a_held, spread, a_sem, out_sem = rest[-5:]
    at_start = lax.axis_index("col") == 0

    @pl.when(at_start if first_column else jnp.logical_not(at_start))
    def _():
        held = a_ref
        if first_column:
            held = a_held
            a_copy = pltpu.make_async_copy(a_ref, a_held, a_sem)
            a_copy.start()
            a_copy.wait()
        total = jnp.zeros((NNZ, LANES), jnp.float32)
        for t in range(PAIRS):
            x = held[0, 0, :, t * LANES : (t + 1) * LANES].astype(jnp.float32)
            total = total + x * x
        row = jnp.sum(total, axis=0, keepdims=True)
        spread[...] = jnp.broadcast_to(row[None], spread.shape)
        out_copy = pltpu.make_async_copy(spread, out_ref, out_sem)
        out_copy.start()
        out_copy.wait()


def after(token, name, limit, width=LANES):
    return pl.pallas_call(
        lambda token_ref, out_ref: None,
        out_shape=pltpu.HBM((8, width), jnp.float32),
        in_specs=[ANY],
        out_specs=ANY,
        compiler_params=pltpu.CompilerParams(vmem_limit_bytes=limit),
        name=name,
    )(pltpu.with_memory_space_constraint(token, pltpu.HBM))


def send_list(slots_ref, step, listed, place, sem):
    left_slot, right_slot, product_slot = (slots_ref[0, 0, kind, step : step + 1] for kind in range(3))
    listed[...] = (right_slot * NNZ + left_slot) * (PAIRS << SHIFT) + product_slot * APART
    copy = pltpu.make_async_copy(listed.at[0], place, sem)
    copy.start()
    return copy


def add_products(a_ref, b_ref, places, arriving, wide, left, pairs, totals):
    for t in range(PAIRS):
        wide[pl.ds(t, NNZ, stride=APART), :] = a_ref[0, 0, :, t * LANES : (t + 1) * LANES].astype(jnp.float32)
    for n in range(NNZ):
        left[n * PAIRS : (n + 1) * PAIRS, :] = wide[n * APART : n * APART + PAIRS, :].astype(jnp.bfloat16)

    low = lax.broadcasted_iota(jnp.int32, (NNZ, LANES), 1) < BS
    for t in range(PAIRS):
        x = b_ref[0, 0, :, t * LANES : (t + 1) * LANES].astype(jnp.float32)
        swapped = pltpu.roll(x, BS, 1)
        wide[pl.ds(2 * t, NNZ, stride=BS + PAD), :] = jnp.where(low, x, swapped)
        wide[pl.ds(2 * t + 1, NNZ, stride=BS + PAD), :] = jnp.where(low, swapped, x)

    side = lax.broadcasted_iota(jnp.int32, (BS, LANES), 1) < BS
    for p in range(NNZ // 2):
        weights = []
        for r in (2 * p, 2 * p + 1):
            x = wide[r * (BS + PAD) : r * (BS + PAD) + BS, :]
            weights.append(
                jnp.concatenate([jnp.where(side, x, 0.0), jnp.where(side, 0.0, x)], axis=0).astype(jnp.bfloat16)
            )
        result = jnp.dot(left[...], jnp.concatenate(weights, axis=1), preferred_element_type=jnp.float32)
        rows = NNZ * PAIRS
        for q in range(2):
            pairs[(2 * p + q) * rows : (2 * p + q + 1) * rows, :] = result[:, q * LANES : (q + 1) * LANES]

    arriving.wait()

    def add_entries(i, carry):
        for u in range(UNROLL):
            place = places[i * UNROLL + u]
            at = pl.multiple_of(lax.shift_right_logical(place, SHIFT), PAIRS)
            to = pl.multiple_of(place & ((1 << SHIFT) - 1), PAD)
            total = totals[u % TOTALS]
            total[pl.ds(to, PAIRS), :] = total[pl.ds(to, PAIRS), :] + pairs[pl.ds(at, PAIRS), :]
        return carry

    lax.fori_loop(0, places.shape[0] // UNROLL, add_entries, 0)


def own_kernel(a_ref, b_ref, slots_ref, *rest):
    totals = rest[:TOTALS]
    listed, place, wide, left, pairs, sem = rest[TOTALS:]
    copy = send_list(slots_ref, 0, listed, place, sem)
    for total in totals:
        total[...] = jnp.zeros_like(total)
    add_products(a_ref, b_ref, place, copy, wide, left, pairs, totals)


def moved_kernel(a_ref, b_ref, slots_ref, *rest):
    _, out_ref, totals = rest[:TOTALS], rest[TOTALS], rest[TOTALS + 1 : 2 * TOTALS + 1]
    listed, place, wide, left, pairs, sem = rest[2 * TOTALS + 1 :]
    copy = send_list(slots_ref, 1, listed, place, sem)
    add_products(a_ref, b_ref, place, copy, wide, left, pairs, totals)

    for c in range(NC):
        rows = slice(c * APART, c * APART + PAIRS)
        totals[0][rows] = (totals[0][rows] + totals[1][rows]) + (totals[2][rows] + totals[3][rows])
    for t in range(PAIRS):
        out_ref[0, 0, :, t * LANES : (t + 1) * LANES] = totals[0][pl.ds(t, NC, stride=APART), :]


def both_products(a_blocks, b_blocks, a_moved, b_moved, products):
    count = products.shape[-1]
    slots = jnp.swapaxes(products, 2, 3)
    total = jax.ShapeDtypeStruct(((NC + 1) * APART, LANES), jnp.float32)
    settings = dict(
        scratch_shapes=[
            pltpu.VMEM((1, count), jnp.int32),
            pltpu.SMEM((count,), jnp.int32),
            pltpu.VMEM((NNZ * (BS + PAD), LANES), jnp.float32),
            pltpu.VMEM((NNZ * PAIRS, LANES), jnp.bfloat16),
            pltpu.VMEM((NNZ * NNZ * PAIRS, LANES), jnp.float32),
            pltpu.SemaphoreType.DMA,
        ],
        compiler_params=pltpu.CompilerParams(vmem_limit_bytes=32 * 1024 * 1024),
        cost_estimate=pl.CostEstimate(flops=6 * 10**8, bytes_accessed=4 * 10**6, transcendentals=0),
    )
    totals = pl.pallas_call(
        own_kernel,
        out_shape=(total,) * TOTALS,
        in_specs=[VMEM] * 3,
        out_specs=(VMEM,) * TOTALS,
        name="own",
        **settings,
    )(a_blocks, b_blocks, slots)
    return pl.pallas_call(
        moved_kernel,
        out_shape=(jax.ShapeDtypeStruct((1, 1, NC, BS * BS), jnp.float32),) + (total,) * TOTALS,
        in_specs=[VMEM] * (3 + TOTALS),
        out_specs=(VMEM,) * (1 + TOTALS),
        input_output_aliases={3 + i: 1 + i for i in range(TOTALS)},
        name="moved",
        **settings,
    )(a_moved, b_moved, slots, *totals)[0]


def squares(a_blocks, count, before=()):
    first_column = not before
    return pl.pallas_call(
        functools.partial(squares_kernel, first_column),
        out_shape=pltpu.HBM((count, 1, LANES), jnp.float32),
        in_specs=[ANY if first_column else VMEM] + [ANY] * len(before),
        out_specs=ANY,
        scratch_shapes=[
            pltpu.VMEM(a_blocks.shape, a_blocks.dtype),
            pltpu.VMEM((count, 1, LANES), jnp.float32),
            pltpu.SemaphoreType.DMA,
            pltpu.SemaphoreType.DMA,
        ],
        input_output_aliases={} if first_column else {1: 0},
        compiler_params=pltpu.CompilerParams(vmem_limit_bytes=FULL_VMEM) if first_column else None,
        name="squares_early" if first_column else "squares_late",
    )(
        pltpu.with_memory_space_constraint(a_blocks, pltpu.HBM if first_column else pltpu.VMEM),
        *(pltpu.with_memory_space_constraint(x, pltpu.HBM) for x in before),
    )


def per_device(a_blocks, b_blocks, products):
    count = lax.axis_size("row") * lax.axis_size("col")
    ready = squares(a_blocks, count)
    first = after(after(ready, "first", FULL_VMEM), "second", FULL_VMEM)
    first, a_after = lax.optimization_barrier((first, a_blocks))
    a_moved = passed_along(a_after, "col", -1)
    third = after(ready, "third", SOME_VMEM, 8192)
    third, b_after = lax.optimization_barrier((third, b_blocks))
    b_moved = passed_along(b_after, "row", -1)
    ready = squares(a_blocks, count, (ready, first, third))
    everyone = lax.all_to_all(ready, ("row", "col"), 0, 0, tiled=True)
    a_near, b_near = (pltpu.with_memory_space_constraint(x, pltpu.VMEM) for x in (a_blocks, b_blocks))
    product = both_products(a_near, b_near, a_moved, b_moved, products)
    everyone, product = lax.optimization_barrier((everyone, product))
    norm_sq = jnp.sum(everyone * jnp.float32(1.0 / (count * NNZ * BS)))
    return (product, norm_sq)


def solution(mesh):
    return jax.shard_map(
        per_device,
        mesh=mesh,
        in_specs=(
            P("row", "col", None, None),
            P("row", "col", None, None),
            P("row", "col", None, None, None),
        ),
        out_specs=(P("row", "col", None, None), P()),
        check_vma=False,
    )
```

```python
import functools

import jax
import jax.numpy as jnp
from jax import lax
from jax.experimental import pallas as pl
from jax.experimental.pallas import tpu as pltpu
from jax.sharding import PartitionSpec as P

BS = 64
NNZ = 24
NC = 32
LANES = 128
PAIRS = BS * BS // LANES
PAD = 8
APART = PAIRS + PAD
UNROLL = 16
TOTALS = 4
SHIFT = 11
FULL_VMEM = 66900000
SOME_VMEM = 16 * 1024 * 1024

VMEM = pl.BlockSpec(memory_space=pltpu.VMEM)
ANY = pl.BlockSpec(memory_space=pl.ANY)


def passed_along(block, axis, distance):
    devices = range(lax.axis_size(axis))
    route = [((i - distance) % len(devices), i) for i in devices]
    return lax.ppermute(block, axis, route)


def squares_kernel(first_column, a_ref, *rest):
    out_ref, a_held, spread, a_sem, out_sem = rest[-5:]
    at_start = lax.axis_index("col") == 0

    @pl.when(at_start if first_column else jnp.logical_not(at_start))
    def _():
        held = a_ref
        if first_column:
            held = a_held
            a_copy = pltpu.make_async_copy(a_ref, a_held, a_sem)
            a_copy.start()
            a_copy.wait()
        total = jnp.zeros((NNZ, LANES), jnp.float32)
        for t in range(PAIRS):
            x = held[0, 0, :, t * LANES : (t + 1) * LANES].astype(jnp.float32)
            total = total + x * x
        row = jnp.sum(total, axis=0, keepdims=True)
        spread[...] = jnp.broadcast_to(row[None], spread.shape)
        out_copy = pltpu.make_async_copy(spread, out_ref, out_sem)
        out_copy.start()
        out_copy.wait()


def after(token, name, limit, width=LANES):
    return pl.pallas_call(
        lambda token_ref, out_ref: None,
        out_shape=pltpu.HBM((8, width), jnp.float32),
        in_specs=[ANY],
        out_specs=ANY,
        compiler_params=pltpu.CompilerParams(vmem_limit_bytes=limit),
        name=name,
    )(pltpu.with_memory_space_constraint(token, pltpu.HBM))


def send_list(slots_ref, step, listed, place, sem):
    left_slot, right_slot, product_slot = (slots_ref[0, 0, kind, step : step + 1] for kind in range(3))
    listed[...] = (right_slot * NNZ + left_slot) * (PAIRS << SHIFT) + product_slot * APART
    copy = pltpu.make_async_copy(listed.at[0], place, sem)
    copy.start()
    behind = lax.broadcasted_iota(jnp.int32, listed.shape, 1) + 1
    used = jnp.max(jnp.where(product_slot < NC, behind, 0))
    return copy, (used + UNROLL - 1) // UNROLL


def add_products(a_ref, b_ref, places, arriving, turns, wide, left, pairs, totals):
    for t in range(PAIRS):
        wide[pl.ds(t, NNZ, stride=APART), :] = a_ref[0, 0, :, t * LANES : (t + 1) * LANES].astype(jnp.float32)
    for n in range(NNZ):
        left[n * PAIRS : (n + 1) * PAIRS, :] = wide[n * APART : n * APART + PAIRS, :].astype(jnp.bfloat16)

    low = lax.broadcasted_iota(jnp.int32, (NNZ, LANES), 1) < BS
    for t in range(PAIRS):
        x = b_ref[0, 0, :, t * LANES : (t + 1) * LANES].astype(jnp.float32)
        swapped = pltpu.roll(x, BS, 1)
        wide[pl.ds(2 * t, NNZ, stride=BS + PAD), :] = jnp.where(low, x, swapped)
        wide[pl.ds(2 * t + 1, NNZ, stride=BS + PAD), :] = jnp.where(low, swapped, x)

    side = lax.broadcasted_iota(jnp.int32, (BS, LANES), 1) < BS
    for p in range(NNZ // 2):
        weights = []
        for r in (2 * p, 2 * p + 1):
            x = wide[r * (BS + PAD) : r * (BS + PAD) + BS, :]
            weights.append(
                jnp.concatenate([jnp.where(side, x, 0.0), jnp.where(side, 0.0, x)], axis=0).astype(jnp.bfloat16)
            )
        result = jnp.dot(left[...], jnp.concatenate(weights, axis=1), preferred_element_type=jnp.float32)
        rows = NNZ * PAIRS
        for q in range(2):
            pairs[(2 * p + q) * rows : (2 * p + q + 1) * rows, :] = result[:, q * LANES : (q + 1) * LANES]

    arriving.wait()

    def add_entries(i, carry):
        for u in range(UNROLL):
            place = places[i * UNROLL + u]
            at = pl.multiple_of(lax.shift_right_logical(place, SHIFT), PAIRS)
            to = pl.multiple_of(place & ((1 << SHIFT) - 1), PAD)
            total = totals[u % TOTALS]
            total[pl.ds(to, PAIRS), :] = total[pl.ds(to, PAIRS), :] + pairs[pl.ds(at, PAIRS), :]
        return carry

    lax.fori_loop(0, turns, add_entries, 0)


def own_kernel(a_ref, b_ref, slots_ref, *rest):
    totals = rest[:TOTALS]
    listed, place, wide, left, pairs, sem = rest[TOTALS:]
    copy, turns = send_list(slots_ref, 0, listed, place, sem)
    for total in totals:
        total[...] = jnp.zeros_like(total)
    add_products(a_ref, b_ref, place, copy, turns, wide, left, pairs, totals)


def moved_kernel(a_ref, b_ref, slots_ref, *rest):
    _, out_ref, totals = rest[:TOTALS], rest[TOTALS], rest[TOTALS + 1 : 2 * TOTALS + 1]
    listed, place, wide, left, pairs, sem = rest[2 * TOTALS + 1 :]
    copy, turns = send_list(slots_ref, 1, listed, place, sem)
    add_products(a_ref, b_ref, place, copy, turns, wide, left, pairs, totals)

    for c in range(NC):
        rows = slice(c * APART, c * APART + PAIRS)
        totals[0][rows] = (totals[0][rows] + totals[1][rows]) + (totals[2][rows] + totals[3][rows])
    for t in range(PAIRS):
        out_ref[0, 0, :, t * LANES : (t + 1) * LANES] = totals[0][pl.ds(t, NC, stride=APART), :]


def both_products(a_blocks, b_blocks, a_moved, b_moved, products):
    count = products.shape[-1]
    slots = jnp.swapaxes(products, 2, 3)
    total = jax.ShapeDtypeStruct(((NC + 1) * APART, LANES), jnp.float32)
    settings = dict(
        scratch_shapes=[
            pltpu.VMEM((1, count), jnp.int32),
            pltpu.SMEM((count,), jnp.int32),
            pltpu.VMEM((NNZ * (BS + PAD), LANES), jnp.float32),
            pltpu.VMEM((NNZ * PAIRS, LANES), jnp.bfloat16),
            pltpu.VMEM((NNZ * NNZ * PAIRS, LANES), jnp.float32),
            pltpu.SemaphoreType.DMA,
        ],
        compiler_params=pltpu.CompilerParams(vmem_limit_bytes=32 * 1024 * 1024),
        cost_estimate=pl.CostEstimate(flops=6 * 10**8, bytes_accessed=4 * 10**6, transcendentals=0),
    )
    totals = pl.pallas_call(
        own_kernel,
        out_shape=(total,) * TOTALS,
        in_specs=[VMEM] * 3,
        out_specs=(VMEM,) * TOTALS,
        name="own",
        **settings,
    )(a_blocks, b_blocks, slots)
    return pl.pallas_call(
        moved_kernel,
        out_shape=(jax.ShapeDtypeStruct((1, 1, NC, BS * BS), jnp.float32),) + (total,) * TOTALS,
        in_specs=[VMEM] * (3 + TOTALS),
        out_specs=(VMEM,) * (1 + TOTALS),
        input_output_aliases={3 + i: 1 + i for i in range(TOTALS)},
        name="moved",
        **settings,
    )(a_moved, b_moved, slots, *totals)[0]


def squares(a_blocks, count, before=()):
    first_column = not before
    return pl.pallas_call(
        functools.partial(squares_kernel, first_column),
        out_shape=pltpu.HBM((count, 1, LANES), jnp.float32),
        in_specs=[ANY if first_column else VMEM] + [ANY] * len(before),
        out_specs=ANY,
        scratch_shapes=[
            pltpu.VMEM(a_blocks.shape, a_blocks.dtype),
            pltpu.VMEM((count, 1, LANES), jnp.float32),
            pltpu.SemaphoreType.DMA,
            pltpu.SemaphoreType.DMA,
        ],
        input_output_aliases={} if first_column else {1: 0},
        compiler_params=pltpu.CompilerParams(vmem_limit_bytes=FULL_VMEM) if first_column else None,
        name="squares_early" if first_column else "squares_late",
    )(
        pltpu.with_memory_space_constraint(a_blocks, pltpu.HBM if first_column else pltpu.VMEM),
        *(pltpu.with_memory_space_constraint(x, pltpu.HBM) for x in before),
    )


def per_device(a_blocks, b_blocks, products):
    count = lax.axis_size("row") * lax.axis_size("col")
    ready = squares(a_blocks, count)
    first = after(after(ready, "first", FULL_VMEM), "second", FULL_VMEM)
    first, a_after = lax.optimization_barrier((first, a_blocks))
    a_moved = passed_along(a_after, "col", -1)
    third = after(ready, "third", SOME_VMEM, 8192)
    third, b_after = lax.optimization_barrier((third, b_blocks))
    b_moved = passed_along(b_after, "row", -1)
    ready = squares(a_blocks, count, (ready, first, third))
    everyone = lax.all_to_all(ready, ("row", "col"), 0, 0, tiled=True)
    a_near, b_near = (pltpu.with_memory_space_constraint(x, pltpu.VMEM) for x in (a_blocks, b_blocks))
    product = both_products(a_near, b_near, a_moved, b_moved, products)
    everyone, product = lax.optimization_barrier((everyone, product))
    norm_sq = jnp.sum(everyone * jnp.float32(1.0 / (count * NNZ * BS)))
    return (product, norm_sq)


def solution(mesh):
    return jax.shard_map(
        per_device,
        mesh=mesh,
        in_specs=(
            P("row", "col", None, None),
            P("row", "col", None, None),
            P("row", "col", None, None, None),
        ),
        out_specs=(P("row", "col", None, None), P()),
        check_vma=False,
    )
```

```python
import functools

import jax
import jax.numpy as jnp
from jax import lax
from jax.experimental import pallas as pl
from jax.experimental.pallas import tpu as pltpu
from jax.sharding import PartitionSpec as P

BS = 64
NNZ = 24
NC = 32
LANES = 128
PAIRS = BS * BS // LANES
PAD = 8
APART = PAIRS + PAD
UNROLL = 16
TOTALS = 4
SHIFT = 11
FULL_VMEM = 66900000
SOME_VMEM = 16 * 1024 * 1024

VMEM = pl.BlockSpec(memory_space=pltpu.VMEM)
ANY = pl.BlockSpec(memory_space=pl.ANY)


def passed_along(block, axis, distance):
    devices = range(lax.axis_size(axis))
    route = [((i - distance) % len(devices), i) for i in devices]
    return lax.ppermute(block, axis, route)


def squares_kernel(first_column, a_ref, *rest):
    out_ref, a_held, spread, a_sem, out_sem = rest[-5:]
    at_start = lax.axis_index("col") == 0

    @pl.when(at_start if first_column else jnp.logical_not(at_start))
    def _():
        held = a_ref
        if first_column:
            held = a_held
            a_copy = pltpu.make_async_copy(a_ref, a_held, a_sem)
            a_copy.start()
            a_copy.wait()
        total = jnp.zeros((NNZ, LANES), jnp.float32)
        for t in range(PAIRS):
            x = held[0, 0, :, t * LANES : (t + 1) * LANES].astype(jnp.float32)
            total = total + x * x
        row = jnp.sum(total, axis=0, keepdims=True)
        spread[...] = jnp.broadcast_to(row[None], spread.shape)
        out_copy = pltpu.make_async_copy(spread, out_ref, out_sem)
        out_copy.start()
        out_copy.wait()


def after(token, name, limit, width=LANES):
    return pl.pallas_call(
        lambda token_ref, out_ref: None,
        out_shape=pltpu.HBM((8, width), jnp.float32),
        in_specs=[ANY],
        out_specs=ANY,
        compiler_params=pltpu.CompilerParams(vmem_limit_bytes=limit),
        name=name,
    )(pltpu.with_memory_space_constraint(token, pltpu.HBM))


def send_list(slots_ref, step, listed, place, sem):
    left_slot, right_slot, product_slot = (slots_ref[0, 0, kind, step : step + 1] for kind in range(3))
    listed[...] = (right_slot * NNZ + left_slot) * (PAIRS << SHIFT) + product_slot * APART
    copy = pltpu.make_async_copy(listed.at[0], place, sem)
    copy.start()
    behind = lax.broadcasted_iota(jnp.int32, listed.shape, 1) + 1
    used = jnp.max(jnp.where(product_slot < NC, behind, 0))
    return copy, (used + UNROLL - 1) // UNROLL


def add_products(a_ref, b_ref, places, arriving, turns, wide, left, pairs, totals):
    for t in range(PAIRS):
        wide[pl.ds(t, NNZ, stride=APART), :] = a_ref[0, 0, :, t * LANES : (t + 1) * LANES].astype(jnp.float32)
    for n in range(NNZ):
        left[n * PAIRS : (n + 1) * PAIRS, :] = wide[n * APART : n * APART + PAIRS, :].astype(jnp.bfloat16)

    low = lax.broadcasted_iota(jnp.int32, (NNZ, LANES), 1) < BS
    for t in range(PAIRS):
        x = b_ref[0, 0, :, t * LANES : (t + 1) * LANES].astype(jnp.float32)
        swapped = pltpu.roll(x, BS, 1)
        wide[pl.ds(2 * t, NNZ, stride=BS + PAD), :] = jnp.where(low, x, swapped)
        wide[pl.ds(2 * t + 1, NNZ, stride=BS + PAD), :] = jnp.where(low, swapped, x)

    side = lax.broadcasted_iota(jnp.int32, (BS, LANES), 1) < BS
    for p in range(NNZ // 2):
        weights = []
        for r in (2 * p, 2 * p + 1):
            x = wide[r * (BS + PAD) : r * (BS + PAD) + BS, :]
            weights.append(
                jnp.concatenate([jnp.where(side, x, 0.0), jnp.where(side, 0.0, x)], axis=0).astype(jnp.bfloat16)
            )
        result = jnp.dot(left[...], jnp.concatenate(weights, axis=1), preferred_element_type=jnp.float32)
        rows = NNZ * PAIRS
        for q in range(2):
            pairs[(2 * p + q) * rows : (2 * p + q + 1) * rows, :] = result[:, q * LANES : (q + 1) * LANES]

    arriving.wait()

    def add_entries(i, carry):
        for u in range(UNROLL):
            place = places[i * UNROLL + u]
            at = pl.multiple_of(lax.shift_right_logical(place, SHIFT), PAIRS)
            to = pl.multiple_of(place & ((1 << SHIFT) - 1), PAD)
            total = totals[u % TOTALS]
            total[pl.ds(to, PAIRS), :] = total[pl.ds(to, PAIRS), :] + pairs[pl.ds(at, PAIRS), :]
        return carry

    lax.fori_loop(0, turns, add_entries, 0)


def own_kernel(a_ref, b_ref, slots_ref, *rest):
    totals = rest[:TOTALS]
    listed, place, wide, left, pairs, sem = rest[TOTALS:]
    copy, turns = send_list(slots_ref, 0, listed, place, sem)
    for total in totals:
        total[...] = jnp.zeros_like(total)
    add_products(a_ref, b_ref, place, copy, turns, wide, left, pairs, totals)


def moved_kernel(a_ref, b_ref, slots_ref, *rest):
    _, out_ref, totals = rest[:TOTALS], rest[TOTALS], rest[TOTALS + 1 : 2 * TOTALS + 1]
    listed, place, wide, left, pairs, sem = rest[2 * TOTALS + 1 :]
    copy, turns = send_list(slots_ref, 1, listed, place, sem)
    add_products(a_ref, b_ref, place, copy, turns, wide, left, pairs, totals)

    for c in range(NC):
        rows = slice(c * APART, c * APART + PAIRS)
        totals[0][rows] = (totals[0][rows] + totals[1][rows]) + (totals[2][rows] + totals[3][rows])
    for t in range(PAIRS):
        out_ref[0, 0, :, t * LANES : (t + 1) * LANES] = totals[0][pl.ds(t, NC, stride=APART), :]


def both_products(a_blocks, b_blocks, a_moved, b_moved, products):
    count = products.shape[-1]
    slots = jnp.swapaxes(products, 2, 3)
    total = jax.ShapeDtypeStruct(((NC + 1) * APART, LANES), jnp.float32)
    settings = dict(
        scratch_shapes=[
            pltpu.VMEM((1, count), jnp.int32),
            pltpu.SMEM((count,), jnp.int32),
            pltpu.VMEM((NNZ * (BS + PAD), LANES), jnp.float32),
            pltpu.VMEM((NNZ * PAIRS, LANES), jnp.bfloat16),
            pltpu.VMEM((NNZ * NNZ * PAIRS, LANES), jnp.float32),
            pltpu.SemaphoreType.DMA,
        ],
        compiler_params=pltpu.CompilerParams(vmem_limit_bytes=32 * 1024 * 1024),
        cost_estimate=pl.CostEstimate(flops=6 * 10**8, bytes_accessed=4 * 10**6, transcendentals=0),
    )
    totals = pl.pallas_call(
        own_kernel,
        out_shape=(total,) * TOTALS,
        in_specs=[VMEM] * 3,
        out_specs=(VMEM,) * TOTALS,
        name="own",
        **settings,
    )(a_blocks, b_blocks, slots)
    return pl.pallas_call(
        moved_kernel,
        out_shape=(jax.ShapeDtypeStruct((1, 1, NC, BS * BS), jnp.float32),) + (total,) * TOTALS,
        in_specs=[VMEM] * (3 + TOTALS),
        out_specs=(VMEM,) * (1 + TOTALS),
        input_output_aliases={3 + i: 1 + i for i in range(TOTALS)},
        name="moved",
        **settings,
    )(a_moved, b_moved, slots, *totals)[0]


def squares(a_blocks, count, before=()):
    first_column = not before
    return pl.pallas_call(
        functools.partial(squares_kernel, first_column),
        out_shape=pltpu.HBM((count, 1, LANES), jnp.float32),
        in_specs=[ANY if first_column else VMEM] + [ANY] * len(before),
        out_specs=ANY,
        scratch_shapes=[
            pltpu.VMEM(a_blocks.shape, a_blocks.dtype),
            pltpu.VMEM((count, 1, LANES), jnp.float32),
            pltpu.SemaphoreType.DMA,
            pltpu.SemaphoreType.DMA,
        ],
        input_output_aliases={} if first_column else {1: 0},
        compiler_params=pltpu.CompilerParams(vmem_limit_bytes=FULL_VMEM) if first_column else None,
        name="squares_early" if first_column else "squares_late",
    )(
        pltpu.with_memory_space_constraint(a_blocks, pltpu.HBM if first_column else pltpu.VMEM),
        *(pltpu.with_memory_space_constraint(x, pltpu.HBM) for x in before),
    )


def per_device(a_blocks, b_blocks, products):
    count = lax.axis_size("row") * lax.axis_size("col")
    ready = squares(a_blocks, count)
    first = after(after(ready, "first", FULL_VMEM), "second", FULL_VMEM)
    first, a_after = lax.optimization_barrier((first, a_blocks))
    a_moved = passed_along(a_after, "col", -1)
    third = after(ready, "third", SOME_VMEM, 49152)
    third, b_after = lax.optimization_barrier((third, b_blocks))
    b_moved = passed_along(b_after, "row", -1)
    ready = squares(a_blocks, count, (ready, first, third))
    everyone = lax.all_to_all(ready, ("row", "col"), 0, 0, tiled=True)
    a_near, b_near = (pltpu.with_memory_space_constraint(x, pltpu.VMEM) for x in (a_blocks, b_blocks))
    product = both_products(a_near, b_near, a_moved, b_moved, products)
    everyone, product = lax.optimization_barrier((everyone, product))
    norm_sq = jnp.sum(everyone * jnp.float32(1.0 / (count * NNZ * BS)))
    return (product, norm_sq)


def solution(mesh):
    return jax.shard_map(
        per_device,
        mesh=mesh,
        in_specs=(
            P("row", "col", None, None),
            P("row", "col", None, None),
            P("row", "col", None, None, None),
        ),
        out_specs=(P("row", "col", None, None), P()),
        check_vma=False,
    )
```

```python
import functools

import jax
import jax.numpy as jnp
from jax import lax
from jax.experimental import pallas as pl
from jax.experimental.pallas import tpu as pltpu
from jax.sharding import PartitionSpec as P

BS = 64
NNZ = 24
NC = 32
LANES = 128
PAIRS = BS * BS // LANES
PAD = 8
APART = PAIRS + PAD
UNROLL = 16
TOTALS = 4
SHIFT = 11
FULL_VMEM = 66900000
SOME_VMEM = 16 * 1024 * 1024

VMEM = pl.BlockSpec(memory_space=pltpu.VMEM)
ANY = pl.BlockSpec(memory_space=pl.ANY)


def passed_along(block, axis, distance):
    devices = range(lax.axis_size(axis))
    route = [((i - distance) % len(devices), i) for i in devices]
    return lax.ppermute(block, axis, route)


def squares_kernel(first_column, a_ref, *rest):
    out_ref, a_held, spread, a_sem, out_sem = rest[-5:]
    at_start = lax.axis_index("col") == 0

    @pl.when(at_start if first_column else jnp.logical_not(at_start))
    def _():
        held = a_ref
        if first_column:
            held = a_held
            a_copy = pltpu.make_async_copy(a_ref, a_held, a_sem)
            a_copy.start()
            a_copy.wait()
        total = jnp.zeros((NNZ, LANES), jnp.float32)
        for t in range(PAIRS):
            x = held[0, 0, :, t * LANES : (t + 1) * LANES].astype(jnp.float32)
            total = total + x * x
        row = jnp.sum(total, axis=0, keepdims=True)
        spread[...] = jnp.broadcast_to(row[None], spread.shape)
        out_copy = pltpu.make_async_copy(spread, out_ref, out_sem)
        out_copy.start()
        out_copy.wait()


def after(token, name, limit, width=LANES):
    return pl.pallas_call(
        lambda token_ref, out_ref: None,
        out_shape=pltpu.HBM((8, width), jnp.float32),
        in_specs=[ANY],
        out_specs=ANY,
        compiler_params=pltpu.CompilerParams(vmem_limit_bytes=limit),
        name=name,
    )(pltpu.with_memory_space_constraint(token, pltpu.HBM))


def send_list(slots_ref, step, listed, place, sem):
    left_slot, right_slot, product_slot = (slots_ref[0, 0, kind, step : step + 1] for kind in range(3))
    listed[...] = (right_slot * NNZ + left_slot) * (PAIRS << SHIFT) + product_slot * APART
    copy = pltpu.make_async_copy(listed.at[0], place, sem)
    copy.start()
    behind = lax.broadcasted_iota(jnp.int32, listed.shape, 1) + 1
    used = jnp.max(jnp.where(product_slot < NC, behind, 0))
    return copy, (used + UNROLL - 1) // UNROLL


def add_products(a_ref, b_ref, places, arriving, turns, wide, left, pairs, totals):
    for t in range(PAIRS):
        wide[pl.ds(t, NNZ, stride=APART), :] = a_ref[0, 0, :, t * LANES : (t + 1) * LANES].astype(jnp.float32)
    for n in range(NNZ):
        left[n * PAIRS : (n + 1) * PAIRS, :] = wide[n * APART : n * APART + PAIRS, :].astype(jnp.bfloat16)

    low = lax.broadcasted_iota(jnp.int32, (NNZ, LANES), 1) < BS
    for t in range(PAIRS):
        x = b_ref[0, 0, :, t * LANES : (t + 1) * LANES].astype(jnp.float32)
        swapped = pltpu.roll(x, BS, 1)
        wide[pl.ds(2 * t, NNZ, stride=BS + PAD), :] = jnp.where(low, x, swapped)
        wide[pl.ds(2 * t + 1, NNZ, stride=BS + PAD), :] = jnp.where(low, swapped, x)

    side = lax.broadcasted_iota(jnp.int32, (BS, LANES), 1) < BS
    for p in range(NNZ // 2):
        weights = []
        for r in (2 * p, 2 * p + 1):
            x = wide[r * (BS + PAD) : r * (BS + PAD) + BS, :]
            weights.append(
                jnp.concatenate([jnp.where(side, x, 0.0), jnp.where(side, 0.0, x)], axis=0).astype(jnp.bfloat16)
            )
        result = jnp.dot(left[...], jnp.concatenate(weights, axis=1), preferred_element_type=jnp.float32)
        rows = NNZ * PAIRS
        for q in range(2):
            pairs[(2 * p + q) * rows : (2 * p + q + 1) * rows, :] = result[:, q * LANES : (q + 1) * LANES]

    arriving.wait()

    def add_entries(i, carry):
        for u in range(UNROLL):
            place = places[i * UNROLL + u]
            at = pl.multiple_of(lax.shift_right_logical(place, SHIFT), PAIRS)
            to = pl.multiple_of(place & ((1 << SHIFT) - 1), PAD)
            total = totals[u % TOTALS]
            total[pl.ds(to, PAIRS), :] = total[pl.ds(to, PAIRS), :] + pairs[pl.ds(at, PAIRS), :]
        return carry

    lax.fori_loop(0, turns, add_entries, 0)


def own_kernel(a_ref, b_ref, slots_ref, *rest):
    totals = rest[:TOTALS]
    listed, place, wide, left, pairs, sem = rest[TOTALS:]
    copy, turns = send_list(slots_ref, 0, listed, place, sem)
    for total in totals:
        total[...] = jnp.zeros_like(total)
    add_products(a_ref, b_ref, place, copy, turns, wide, left, pairs, totals)


def moved_kernel(a_ref, b_ref, slots_ref, *rest):
    _, out_ref, totals = rest[:TOTALS], rest[TOTALS], rest[TOTALS + 1 : 2 * TOTALS + 1]
    listed, place, wide, left, pairs, sem = rest[2 * TOTALS + 1 :]
    copy, turns = send_list(slots_ref, 1, listed, place, sem)
    add_products(a_ref, b_ref, place, copy, turns, wide, left, pairs, totals)

    for c in range(NC):
        rows = slice(c * APART, c * APART + PAIRS)
        totals[0][rows] = (totals[0][rows] + totals[1][rows]) + (totals[2][rows] + totals[3][rows])
    for t in range(PAIRS):
        out_ref[0, 0, :, t * LANES : (t + 1) * LANES] = totals[0][pl.ds(t, NC, stride=APART), :]


def both_products(a_blocks, b_blocks, a_moved, b_moved, products):
    count = products.shape[-1]
    slots = jnp.swapaxes(products, 2, 3)
    total = jax.ShapeDtypeStruct(((NC + 1) * APART, LANES), jnp.float32)
    settings = dict(
        scratch_shapes=[
            pltpu.VMEM((1, count), jnp.int32),
            pltpu.SMEM((count,), jnp.int32),
            pltpu.VMEM((NNZ * (BS + PAD), LANES), jnp.float32),
            pltpu.VMEM((NNZ * PAIRS, LANES), jnp.bfloat16),
            pltpu.VMEM((NNZ * NNZ * PAIRS, LANES), jnp.float32),
            pltpu.SemaphoreType.DMA,
        ],
        compiler_params=pltpu.CompilerParams(vmem_limit_bytes=32 * 1024 * 1024),
        cost_estimate=pl.CostEstimate(flops=6 * 10**8, bytes_accessed=4 * 10**6, transcendentals=0),
    )
    totals = pl.pallas_call(
        own_kernel,
        out_shape=(total,) * TOTALS,
        in_specs=[VMEM] * 3,
        out_specs=(VMEM,) * TOTALS,
        name="own",
        **settings,
    )(a_blocks, b_blocks, slots)
    return pl.pallas_call(
        moved_kernel,
        out_shape=(jax.ShapeDtypeStruct((1, 1, NC, BS * BS), jnp.float32),) + (total,) * TOTALS,
        in_specs=[VMEM] * (3 + TOTALS),
        out_specs=(VMEM,) * (1 + TOTALS),
        input_output_aliases={3 + i: 1 + i for i in range(TOTALS)},
        name="moved",
        **settings,
    )(a_moved, b_moved, slots, *totals)[0]


def squares(a_blocks, count, before=()):
    first_column = not before
    return pl.pallas_call(
        functools.partial(squares_kernel, first_column),
        out_shape=pltpu.HBM((count, 1, LANES), jnp.float32),
        in_specs=[ANY if first_column else VMEM] + [ANY] * len(before),
        out_specs=ANY,
        scratch_shapes=[
            pltpu.VMEM(a_blocks.shape, a_blocks.dtype),
            pltpu.VMEM((count, 1, LANES), jnp.float32),
            pltpu.SemaphoreType.DMA,
            pltpu.SemaphoreType.DMA,
        ],
        input_output_aliases={} if first_column else {1: 0},
        compiler_params=pltpu.CompilerParams(vmem_limit_bytes=FULL_VMEM) if first_column else None,
        name="squares_early" if first_column else "squares_late",
    )(
        pltpu.with_memory_space_constraint(a_blocks, pltpu.HBM if first_column else pltpu.VMEM),
        *(pltpu.with_memory_space_constraint(x, pltpu.HBM) for x in before),
    )


def per_device(a_blocks, b_blocks, products):
    count = lax.axis_size("row") * lax.axis_size("col")
    ready = squares(a_blocks, count)
    ready, a_after = lax.optimization_barrier((ready, a_blocks))
    a_moved = passed_along(a_after, "col", -1)
    third = after(ready, "third", SOME_VMEM, 49152)
    b_moved = passed_along(b_blocks, "row", -1)
    ready = squares(a_blocks, count, (ready, third))
    everyone = lax.all_to_all(ready, ("row", "col"), 0, 0, tiled=True)
    a_near, b_near = (pltpu.with_memory_space_constraint(x, pltpu.VMEM) for x in (a_blocks, b_blocks))
    product = both_products(a_near, b_near, a_moved, b_moved, products)
    everyone, product = lax.optimization_barrier((everyone, product))
    norm_sq = jnp.sum(everyone * jnp.float32(1.0 / (count * NNZ * BS)))
    return (product, norm_sq)


def solution(mesh):
    return jax.shard_map(
        per_device,
        mesh=mesh,
        in_specs=(
            P("row", "col", None, None),
            P("row", "col", None, None),
            P("row", "col", None, None, None),
        ),
        out_specs=(P("row", "col", None, None), P()),
        check_vma=False,
    )
```

```python
import functools

import jax
import jax.numpy as jnp
from jax import lax
from jax.experimental import pallas as pl
from jax.experimental.pallas import tpu as pltpu
from jax.sharding import PartitionSpec as P

BS = 64
NNZ = 24
NC = 32
LANES = 128
PAIRS = BS * BS // LANES
PAD = 8
APART = PAIRS + PAD
UNROLL = 16
TOTALS = 4
SHIFT = 11
FULL_VMEM = 66900000
SOME_VMEM = 16 * 1024 * 1024

VMEM = pl.BlockSpec(memory_space=pltpu.VMEM)
ANY = pl.BlockSpec(memory_space=pl.ANY)


def passed_along(block, axis, distance):
    devices = range(lax.axis_size(axis))
    route = [((i - distance) % len(devices), i) for i in devices]
    return lax.ppermute(block, axis, route)


def squares_kernel(first_column, a_ref, *rest):
    out_ref, a_held, spread, a_sem, out_sem = rest[-5:]
    at_start = lax.axis_index("col") == 0

    @pl.when(at_start if first_column else jnp.logical_not(at_start))
    def _():
        held = a_ref
        if first_column:
            held = a_held
            a_copy = pltpu.make_async_copy(a_ref, a_held, a_sem)
            a_copy.start()
            a_copy.wait()
        total = jnp.zeros((NNZ, LANES), jnp.float32)
        for t in range(PAIRS):
            x = held[0, 0, :, t * LANES : (t + 1) * LANES].astype(jnp.float32)
            total = total + x * x
        row = jnp.sum(total, axis=0, keepdims=True)
        spread[...] = jnp.broadcast_to(row[None], spread.shape)
        out_copy = pltpu.make_async_copy(spread, out_ref, out_sem)
        out_copy.start()
        out_copy.wait()


def after(token, name, limit, width=LANES):
    return pl.pallas_call(
        lambda token_ref, out_ref: None,
        out_shape=pltpu.HBM((8, width), jnp.float32),
        in_specs=[ANY],
        out_specs=ANY,
        compiler_params=pltpu.CompilerParams(vmem_limit_bytes=limit),
        name=name,
    )(pltpu.with_memory_space_constraint(token, pltpu.HBM))


def send_list(slots_ref, step, listed, place, sem):
    left_slot, right_slot, product_slot = (slots_ref[0, 0, kind, step : step + 1] for kind in range(3))
    listed[...] = (right_slot * NNZ + left_slot) * (PAIRS << SHIFT) + product_slot * APART
    copy = pltpu.make_async_copy(listed.at[0], place, sem)
    copy.start()
    behind = lax.broadcasted_iota(jnp.int32, listed.shape, 1) + 1
    used = jnp.max(jnp.where(product_slot < NC, behind, 0))
    return copy, (used + UNROLL - 1) // UNROLL


def add_products(a_ref, b_ref, places, arriving, turns, wide, left, pairs, totals):
    for t in range(PAIRS):
        wide[pl.ds(t, NNZ, stride=APART), :] = a_ref[0, 0, :, t * LANES : (t + 1) * LANES].astype(jnp.float32)
    for n in range(NNZ):
        left[n * PAIRS : (n + 1) * PAIRS, :] = wide[n * APART : n * APART + PAIRS, :].astype(jnp.bfloat16)

    low = lax.broadcasted_iota(jnp.int32, (NNZ, LANES), 1) < BS
    for t in range(PAIRS):
        x = b_ref[0, 0, :, t * LANES : (t + 1) * LANES].astype(jnp.float32)
        swapped = pltpu.roll(x, BS, 1)
        wide[pl.ds(2 * t, NNZ, stride=BS + PAD), :] = jnp.where(low, x, swapped)
        wide[pl.ds(2 * t + 1, NNZ, stride=BS + PAD), :] = jnp.where(low, swapped, x)

    side = lax.broadcasted_iota(jnp.int32, (BS, LANES), 1) < BS
    for p in range(NNZ // 2):
        weights = []
        for r in (2 * p, 2 * p + 1):
            x = wide[r * (BS + PAD) : r * (BS + PAD) + BS, :]
            weights.append(
                jnp.concatenate([jnp.where(side, x, 0.0), jnp.where(side, 0.0, x)], axis=0).astype(jnp.bfloat16)
            )
        result = jnp.dot(left[...], jnp.concatenate(weights, axis=1), preferred_element_type=jnp.float32)
        rows = NNZ * PAIRS
        for q in range(2):
            pairs[(2 * p + q) * rows : (2 * p + q + 1) * rows, :] = result[:, q * LANES : (q + 1) * LANES]

    arriving.wait()

    def add_entries(i, carry):
        for u in range(UNROLL):
            place = places[i * UNROLL + u]
            at = pl.multiple_of(lax.shift_right_logical(place, SHIFT), PAIRS)
            to = pl.multiple_of(place & ((1 << SHIFT) - 1), PAD)
            total = totals[u % TOTALS]
            total[pl.ds(to, PAIRS), :] = total[pl.ds(to, PAIRS), :] + pairs[pl.ds(at, PAIRS), :]
        return carry

    lax.fori_loop(0, turns, add_entries, 0)


def own_kernel(a_ref, b_ref, slots_ref, *rest):
    totals = rest[:TOTALS]
    listed, place, wide, left, pairs, sem = rest[TOTALS:]
    copy, turns = send_list(slots_ref, 0, listed, place, sem)
    for total in totals:
        for c in range(NC + 1):
            total[c * APART : c * APART + PAIRS, :] = jnp.zeros((PAIRS, LANES), jnp.float32)
    add_products(a_ref, b_ref, place, copy, turns, wide, left, pairs, totals)


def moved_kernel(a_ref, b_ref, slots_ref, *rest):
    _, out_ref, totals = rest[:TOTALS], rest[TOTALS], rest[TOTALS + 1 : 2 * TOTALS + 1]
    listed, place, wide, left, pairs, sem = rest[2 * TOTALS + 1 :]
    copy, turns = send_list(slots_ref, 1, listed, place, sem)
    add_products(a_ref, b_ref, place, copy, turns, wide, left, pairs, totals)

    for c in range(NC):
        rows = slice(c * APART, c * APART + PAIRS)
        totals[0][rows] = (totals[0][rows] + totals[1][rows]) + (totals[2][rows] + totals[3][rows])
    for t in range(PAIRS):
        out_ref[0, 0, :, t * LANES : (t + 1) * LANES] = totals[0][pl.ds(t, NC, stride=APART), :]


def both_products(a_blocks, b_blocks, a_moved, b_moved, products):
    count = products.shape[-1]
    slots = jnp.swapaxes(products, 2, 3)
    total = jax.ShapeDtypeStruct(((NC + 1) * APART, LANES), jnp.float32)
    settings = dict(
        scratch_shapes=[
            pltpu.VMEM((1, count), jnp.int32),
            pltpu.SMEM((count,), jnp.int32),
            pltpu.VMEM((NNZ * (BS + PAD), LANES), jnp.float32),
            pltpu.VMEM((NNZ * PAIRS, LANES), jnp.bfloat16),
            pltpu.VMEM((NNZ * NNZ * PAIRS, LANES), jnp.float32),
            pltpu.SemaphoreType.DMA,
        ],
        compiler_params=pltpu.CompilerParams(vmem_limit_bytes=32 * 1024 * 1024),
        cost_estimate=pl.CostEstimate(flops=6 * 10**8, bytes_accessed=4 * 10**6, transcendentals=0),
    )
    totals = pl.pallas_call(
        own_kernel,
        out_shape=(total,) * TOTALS,
        in_specs=[VMEM] * 3,
        out_specs=(VMEM,) * TOTALS,
        name="own",
        **settings,
    )(a_blocks, b_blocks, slots)
    return pl.pallas_call(
        moved_kernel,
        out_shape=(jax.ShapeDtypeStruct((1, 1, NC, BS * BS), jnp.float32),) + (total,) * TOTALS,
        in_specs=[VMEM] * (3 + TOTALS),
        out_specs=(VMEM,) * (1 + TOTALS),
        input_output_aliases={3 + i: 1 + i for i in range(TOTALS)},
        name="moved",
        **settings,
    )(a_moved, b_moved, slots, *totals)[0]


def squares(a_blocks, count, before=()):
    first_column = not before
    return pl.pallas_call(
        functools.partial(squares_kernel, first_column),
        out_shape=pltpu.HBM((count, 1, LANES), jnp.float32),
        in_specs=[ANY if first_column else VMEM] + [ANY] * len(before),
        out_specs=ANY,
        scratch_shapes=[
            pltpu.VMEM(a_blocks.shape, a_blocks.dtype),
            pltpu.VMEM((count, 1, LANES), jnp.float32),
            pltpu.SemaphoreType.DMA,
            pltpu.SemaphoreType.DMA,
        ],
        input_output_aliases={} if first_column else {1: 0},
        compiler_params=pltpu.CompilerParams(vmem_limit_bytes=FULL_VMEM) if first_column else None,
        name="squares_early" if first_column else "squares_late",
    )(
        pltpu.with_memory_space_constraint(a_blocks, pltpu.HBM if first_column else pltpu.VMEM),
        *(pltpu.with_memory_space_constraint(x, pltpu.HBM) for x in before),
    )


def per_device(a_blocks, b_blocks, products):
    count = lax.axis_size("row") * lax.axis_size("col")
    ready = squares(a_blocks, count)
    ready, a_after = lax.optimization_barrier((ready, a_blocks))
    a_moved = passed_along(a_after, "col", -1)
    third = after(ready, "third", SOME_VMEM, 49152)
    b_moved = passed_along(b_blocks, "row", -1)
    ready = squares(a_blocks, count, (ready, third))
    everyone = lax.all_to_all(ready, ("row", "col"), 0, 0, tiled=True)
    a_near, b_near = (pltpu.with_memory_space_constraint(x, pltpu.VMEM) for x in (a_blocks, b_blocks))
    product = both_products(a_near, b_near, a_moved, b_moved, products)
    everyone, product = lax.optimization_barrier((everyone, product))
    norm_sq = jnp.sum(everyone * jnp.float32(1.0 / (count * NNZ * BS)))
    return (product, norm_sq)


def solution(mesh):
    return jax.shard_map(
        per_device,
        mesh=mesh,
        in_specs=(
            P("row", "col", None, None),
            P("row", "col", None, None),
            P("row", "col", None, None, None),
        ),
        out_specs=(P("row", "col", None, None), P()),
        check_vma=False,
    )
```
